256 devices in a mesh: lat: 8 (over x, z_lo), lon: 32 (over z_hi, y, core).
Axes of the slice: x: 4, y: 4, z: 8 (z_hi: 4, z_lo: 2; z = z_hi * 2 + z_lo), core: 2. Of those that a mesh axis runs over, the one named last changes fastest.
Arguments:
- field: float32 [4096, 8192], P('lat', 'lon'), may hold values from -6 to 6
- tapers: bfloat16 [4, 4096, 8192], P(None, 'lat', 'lon'), may hold values from 0.19921875 to 1
- orders: int32 [128], replicated, may hold values from 0 to 2303, as said below
- legendre: bfloat16 [128, 4096, 2304], P('lon', 'lat')
Outputs:
- coeffs: float32 [4, 128, 2, 2304], P(None, 'lon', None, 'lat')
The draws below stay inside these ranges and needn't reach their ends.
Inputs may be any that keep to these rules, and one draw needn't show every extreme that they name: Distinct orders, 0 and 2303 among them; slots j * 4 to (j + 1) * 4 - 1 belong to longitude sector j; legendre[j, t, l] is zero where l < orders[j].
All inputs are finite; a program needn't handle non-finite values.
Results may differ from the reference program's by a relative error of at most 0.0047.
Values may be sent and summed in bfloat16 or wider, within the bound.
No kernel may reach another device: no remote copies, remote signals or barrier semaphores. Data moves between devices by JAX's collectives and lax.ppermute only.
A program may use at most 64 MiB of HBM per device.

```python
import math
import jax
import jax.numpy as jnp
from jax import lax

NLAT = 4096
NLON = 8192
NDEG = 2304
TAPERS = 4
ORDERS = 128


def order_set(key):
    inner_key = jax.random.fold_in(key, 11)
    mixed_key = jax.random.fold_in(key, 12)
    inner = jax.random.permutation(inner_key, NDEG - 2)[:ORDERS - 2] + 1
    edges = jnp.array([0, NDEG - 1], dtype=jnp.int32)
    chosen = jnp.concatenate([edges, inner.astype(jnp.int32)])
    return jax.random.permutation(mixed_key, chosen).astype(jnp.int32)


def draw_orders(key, part):
    return order_set(key)


def draw_legendre(key, part):
    chosen = order_set(key)
    key = jax.random.fold_in(key, 5)
    scale = 2.2 / (NLAT * NLON) ** 0.5
    values = jax.random.normal(key, (ORDERS, NLAT, NDEG), jnp.float32)
    degrees = jnp.arange(NDEG, dtype=jnp.int32)
    keep = (degrees[None, None, :] >= chosen[:, None, None]).astype(jnp.float32)
    return (values * keep * scale).astype(jnp.bfloat16)


def shard_levels(own_key, extent, pieces, least, high):
    def one(axis_at, blocks):
        heights = jax.random.uniform(jax.random.fold_in(jax.random.fold_in(own_key, 6), axis_at), (blocks,), jnp.float32, least / len(pieces), high / len(pieces))
        return jnp.repeat(jnp.exp(heights), extent[axis_at] // blocks).reshape((-1,) + (1,) * (len(extent) - axis_at - 1))

    factor_of = one(*pieces[0])
    for cut in pieces[1:]:
        factor_of = factor_of * one(*cut)
    return factor_of


def centred(stream_key, dims, deviation, bound, cuts=(), held_as=jnp.bfloat16):
    values = jax.random.normal(stream_key, dims, jnp.float32) * deviation
    if len(cuts) > 0:
        values = shard_levels(stream_key, dims, cuts, -0.22, 0.18) * values
    return jnp.clip(values, min=-bound, max=bound).astype(held_as)


def setup_inputs(seed: int = 0) -> dict:
    key_of = jax.random.split(jax.random.key(seed), 5)
    return {
        "field": centred(key_of[0], (NLAT, NLON), 1.0, 6.0, ((0, 8), (1, 32)), jnp.float32),
        "tapers": jnp.clip(0.19921875 + 0.80078125 * jax.random.uniform(key_of[1], (TAPERS, NLAT, NLON), jnp.float32) ** shard_levels(key_of[1], (TAPERS, NLAT, NLON), ((1, 8), (2, 32)), -0.2, 0.2), 0.19921875, 1.0).astype(jnp.bfloat16),
        "orders": draw_orders(jax.random.fold_in(key_of[4], 71), 0),
        "legendre": draw_legendre(jax.random.fold_in(key_of[4], 71), 0),
    }


def trig_table(orders, longitudes, cycle):
    spins = (orders[None, :] * longitudes[:, None]) % cycle
    angle = spins.astype(jnp.float32) * (2.0 * math.pi / cycle)
    table = jnp.stack([jnp.cos(angle), -jnp.sin(angle)], axis=-1)
    return table.reshape(longitudes.shape[0], -1).astype(jnp.bfloat16)


def reference(field, tapers, orders, legendre):
    longitudes = jnp.arange(NLON, dtype=jnp.int32)
    trig = trig_table(orders, longitudes, NLON)
    tapered = (field[None, :, :] * tapers.astype(jnp.float32)).astype(jnp.bfloat16)
    fourier = jnp.dot(tapered.reshape(TAPERS * NLAT, NLON), trig, preferred_element_type=jnp.float32)
    fourier = fourier.astype(jnp.bfloat16).reshape(TAPERS, NLAT, ORDERS, 2)

    def one_order(slot):
        left = lax.dynamic_index_in_dim(fourier, slot, 2, keepdims=False)
        left = jnp.transpose(left, (0, 2, 1)).reshape(TAPERS * 2, NLAT)
        table = lax.dynamic_index_in_dim(legendre, slot, 0, keepdims=False)
        return jnp.dot(left, table, preferred_element_type=jnp.float32).reshape(TAPERS, 2, NDEG)

    coeffs = lax.map(one_order, jnp.arange(ORDERS, dtype=jnp.int32))
    return jnp.transpose(coeffs, (1, 0, 2, 3))
```

```python
import math

import jax
import jax.numpy as jnp
from jax import lax
from jax.experimental import pallas as pl
from jax.experimental.pallas import tpu as pltpu
from jax.sharding import PartitionSpec as P

NLON = 8192
CORES = 2
VMEM_BYTES = 12 * 1024 * 1024


def contract_last(a, b):
    return lax.dot_general(a, b, (((1,), (1,)), ((), ())), preferred_element_type=jnp.float32)


def trig_rows(slots, start, count):
    longitudes = start + jnp.arange(count, dtype=jnp.int32)
    turns = slots[:, None, None] * longitudes[None, None, :]
    turns = turns + (NLON // 4) * jnp.arange(2, dtype=jnp.int32)[None, :, None]
    angle = (turns % NLON).astype(jnp.float32) * (2.0 * math.pi / NLON)
    return jnp.cos(angle).astype(jnp.bfloat16).reshape(-1, count)


def fourier_kernel(trig_own, trig_other, own, other, out):
    chips, _, lats = out.shape
    for pair in range(own.shape[0] // 2):
        parts = []
        for k in (2 * pair, 2 * pair + 1):
            terms = contract_last(trig_own[...], own[k]) + contract_last(trig_other[...], other[k])
            parts.append(terms.reshape(chips, -1, lats))
        block = jnp.concatenate(parts, axis=1)
        rows = block.shape[1]
        out[:, pair * rows:(pair + 1) * rows, :] = block.astype(out.dtype)


def legendre_kernel(pieces, legendre, out, whole):
    orders, _, degrees = legendre.shape
    total = jnp.sum(pieces[...].astype(jnp.float32), axis=0)
    slot = lax.broadcasted_iota(jnp.int32, total.shape, 0) // 2 % orders
    lefts = [jnp.where(slot == i, total, 0.0).astype(jnp.bfloat16) for i in range(orders)]
    width = 768
    for at in range(0, degrees, width):
        acc = None
        for i in range(orders):
            term = jnp.dot(lefts[i], legendre[i, :, at:at + width], preferred_element_type=jnp.float32)
            acc = term if acc is None else acc + term
        whole[:, at:at + width] = acc
    share = out.shape[2]
    for band in range(out.shape[0]):
        out[band] = whole[:, band * share:(band + 1) * share]


def sum_kernel(parts, out):
    total = jnp.sum(parts[...], axis=0)
    for k in range(out.shape[0]):
        for i in range(out.shape[1]):
            row = 2 * (k * out.shape[1] + i)
            out[k, i] = total[row:row + 2, :]


def call(kernel, out_shape, *operands, scratch=()):
    return pl.pallas_call(
        kernel,
        out_shape=out_shape,
        in_specs=[pl.BlockSpec(memory_space=pltpu.VMEM)] * len(operands),
        out_specs=pl.BlockSpec(memory_space=pltpu.VMEM),
        scratch_shapes=list(scratch),
        compiler_params=pltpu.CompilerParams(vmem_limit_bytes=VMEM_BYTES),
    )(*operands)


def per_device(sectors, bands, field, tapers, orders, legendre):
    num_tapers, lats, lons = tapers.shape
    own_orders, _, degrees = legendre.shape
    chips = sectors // CORES
    me = lax.axis_index("lon")
    chip, core = me // CORES, me % CORES

    tapered = (field[None, :, :] * tapers.astype(jnp.float32)).astype(jnp.bfloat16)
    other = lax.ppermute(tapered, "lon", [(s, s ^ 1) for s in range(sectors)])

    slots = lax.dynamic_index_in_dim(orders.reshape(chips, CORES, own_orders), core, 1, keepdims=False).reshape(-1)
    trig_own = trig_rows(slots, me * lons, lons)
    trig_other = trig_rows(slots, (me ^ 1) * lons, lons)

    rows = num_tapers * own_orders * 2
    terms = call(
        fourier_kernel,
        jax.ShapeDtypeStruct((chips, rows, lats), jnp.bfloat16),
        trig_own, trig_other, tapered, other,
    )
    same_core = [[CORES * q + c for q in range(chips)] for c in range(CORES)]
    pieces = lax.all_to_all(terms, "lon", 0, 0, tiled=True, axis_index_groups=same_core)

    partial_sums = call(
        legendre_kernel,
        jax.ShapeDtypeStruct((bands, rows, degrees // bands), jnp.float32),
        pieces, legendre,
        scratch=[pltpu.VMEM((rows, degrees), jnp.float32)],
    )
    parts = lax.all_to_all(partial_sums, "lat", 0, 0, tiled=True)
    return call(
        sum_kernel,
        jax.ShapeDtypeStruct((num_tapers, own_orders, 2, degrees // bands), jnp.float32),
        parts,
    )


def solution(mesh):
    sectors, bands = mesh.shape["lon"], mesh.shape["lat"]

    def body(field, tapers, orders, legendre):
        return per_device(sectors, bands, field, tapers, orders, legendre)

    return jax.shard_map(
        body,
        mesh=mesh,
        in_specs=(P("lat", "lon"), P(None, "lat", "lon"), P(), P("lon", "lat", None)),
        out_specs=P(None, "lon", None, "lat"),
        check_vma=False,
    )
```

```python
import functools
import math

import jax
import jax.numpy as jnp
from jax import lax
from jax.experimental import pallas as pl
from jax.experimental.pallas import tpu as pltpu
from jax.sharding import PartitionSpec as P

NLON = 8192
CORES = 2
SIDE = 4
YSTEPS = (2, 1, 3)
ZSTEPS = (2, 1, 3)
VMEM_BYTES = 12 * 1024 * 1024
SIN = [(-1.0) ** n / math.factorial(2 * n + 1) for n in range(6)]


def y_of(y, k):
    return (y + k) % SIDE


def z_of(z, k):
    return (z + k) % SIDE


def contract_last(a, b):
    return lax.dot_general(a, b, (((1,), (1,)), ((), ())), preferred_element_type=jnp.float32)


def first_kernel(field, tapers, orders, out, own, other, field_here, tapers_here, orders_here, sems):
    half = out.shape[0] // 2
    parts = [(orders, orders_here), (field, field_here)]
    parts += [(tapers.at[at:at + half], tapers_here.at[at:at + half]) for at in (0, half)]
    copies = [pltpu.make_async_copy(a, b, sems.at[n]) for n, (a, b) in enumerate(parts)]
    for copy in copies:
        copy.start()
    copies[0].wait()
    trig_tables(orders_here, own, other)
    copies[1].wait()
    for k in range(out.shape[0]):
        if k % half == 0:
            copies[2 + k // half].wait()
        out[k] = (field_here[...] * tapers_here[k].astype(jnp.float32)).astype(out.dtype)


def trig_tables(orders, own, other):
    rows, lons = own.shape
    me = lax.axis_index("lon")
    z, y, core = me // (SIDE * CORES), me // CORES % SIDE, me % CORES
    row = lax.broadcasted_iota(jnp.int32, (rows, orders.shape[1]), 0)
    lane = lax.broadcasted_iota(jnp.int32, (rows, orders.shape[1]), 1)
    chip = z_of(z, row // 8 % SIDE) * SIDE + y_of(y, row // 32)
    slot = (chip * CORES + core) * 4 + row // 2 % 4
    picked = jnp.where(lane == slot, orders[...].astype(jnp.float32), 0.0)
    order = jnp.sum(picked, axis=1, keepdims=True).astype(jnp.int32)
    quarter = lax.broadcasted_iota(jnp.int32, (rows, lons), 0) % 2 * (NLON // 4)
    step = lax.broadcasted_iota(jnp.int32, (rows, lons), 1)
    for out, sector in ((own, me), (other, me ^ 1)):
        turn = (order * (sector * lons + step) + quarter) & (NLON - 1)
        arc = (NLON // 4 - jnp.minimum(turn, NLON - turn)).astype(jnp.float32) * (2.0 * math.pi / NLON)
        square = arc * arc
        value = jnp.full_like(arc, SIN[-1])
        for c in SIN[-2::-1]:
            value = value * square + c
        out[...] = (value * arc).astype(out.dtype)


def blocks(trig, tapered, pair):
    lats = tapered.shape[1]
    parts = [contract_last(trig[...], tapered[2 * pair + k]).reshape(SIDE * SIDE, -1, lats) for k in range(2)]
    return jnp.concatenate(parts, axis=1)


def own_kernel(trig, tapered, out):
    for pair in range(tapered.shape[0] // 2):
        out[:, pair * 16:pair * 16 + 16, :] = blocks(trig, tapered, pair)


def other_kernel(trig, tapered, acc, *outs):
    for pair in range(tapered.shape[0] // 2):
        rows = slice(pair * 16, pair * 16 + 16)
        block = blocks(trig, tapered, pair) + acc[:, rows, :]
        for k, out in enumerate(outs):
            out[:, rows, :] = block[SIDE * k:SIDE * k + SIDE].astype(out.dtype)


def add_kernel(own, *refs):
    got, outs = refs[:-SIDE], refs[-SIDE:]
    total = own[...]
    for piece in got:
        total = total + piece[...].astype(jnp.float32)
    for k, out in enumerate(outs):
        out[...] = total[k].astype(out.dtype)


def legendre_kernel(own, *refs):
    got, (legendre, out, whole) = refs[:-3], refs[-3:]
    orders, _, degrees = legendre.shape
    total = own[...]
    for piece in got:
        total = total + piece[...].astype(jnp.float32)
    slot = lax.broadcasted_iota(jnp.int32, total.shape, 0) // 2 % orders
    lefts = [jnp.where(slot == i, total, 0.0).astype(jnp.bfloat16) for i in range(orders)]
    width = 768
    for at in range(0, degrees, width):
        acc = None
        for i in range(orders):
            term = jnp.dot(lefts[i], legendre[i, :, at:at + width], preferred_element_type=jnp.float32)
            acc = term if acc is None else acc + term
        whole[:, at:at + width] = acc
    share = out.shape[2]
    for band in range(out.shape[0]):
        out[band] = whole[:, band * share:(band + 1) * share].astype(out.dtype)


def sum_kernel(parts, out):
    total = jnp.sum(parts[...].astype(jnp.float32), axis=0)
    for k in range(out.shape[0]):
        for i in range(out.shape[1]):
            row = 2 * (k * out.shape[1] + i)
            out[k, i] = total[row:row + 2, :]


def call(kernel, out_shape, *operands, scratch=(), us=2, space=pltpu.VMEM):
    spec = pl.BlockSpec(memory_space=pltpu.VMEM)
    return pl.pallas_call(
        kernel,
        out_shape=out_shape,
        in_specs=[pl.BlockSpec(memory_space=space)] * len(operands),
        out_specs=[spec] * len(out_shape) if isinstance(out_shape, list) else spec,
        scratch_shapes=list(scratch),
        compiler_params=pltpu.CompilerParams(vmem_limit_bytes=VMEM_BYTES),
        cost_estimate=pl.CostEstimate(flops=us * 10**9, bytes_accessed=us * 3 * 10**6, transcendentals=0),
    )(*operands)


def pairs(step):
    at = lambda z, y, c: (z * SIDE + y) * CORES + c
    return [(at(z, y, c), at(*step(z, y, c))) for z in range(SIDE) for y in range(SIDE) for c in range(CORES)]


def per_device(bands, field, tapers, orders, legendre):
    num_tapers, lats, lons = tapers.shape
    own_orders, _, degrees = legendre.shape
    rows = num_tapers * own_orders * 2
    shape = jax.ShapeDtypeStruct
    bf16, f32 = jnp.bfloat16, jnp.float32

    wide = shape((SIDE * SIDE * own_orders * 2, lons), bf16)
    tapered, trig_own, trig_other = call(
        first_kernel, [shape(tapers.shape, bf16), wide, wide],
        *[pltpu.with_memory_space_constraint(a, pltpu.HBM) for a in (field, tapers, orders.reshape(1, -1))],
        scratch=[
            pltpu.VMEM(field.shape, f32), pltpu.VMEM(tapers.shape, bf16), pltpu.VMEM((1, orders.shape[0]), jnp.int32),
            pltpu.SemaphoreType.DMA((4,)),
        ],
        us=1, space=pltpu.HBM,
    )
    other = lax.ppermute(tapered, "lon", pairs(lambda z, y, c: (z, y, 1 - c)))
    acc = call(own_kernel, shape((SIDE * SIDE, rows, lats), f32), trig_own, tapered, us=1)
    plane = (SIDE, rows, lats)
    sums = call(other_kernel, [shape(plane, f32)] + [shape(plane, bf16)] * 3, trig_other, other, acc, us=1)
    got = [lax.ppermute(sums[k], "lon", pairs(lambda z, y, c, k=k: (z, y_of(y, k), c))) for k in YSTEPS]
    block = (rows, lats)
    sums = call(add_kernel, [shape(block, f32)] + [shape(block, bf16)] * 3, sums[0], *got, us=1)
    got = [lax.ppermute(sums[k], "lon", pairs(lambda z, y, c, k=k: (z_of(z, k), y, c))) for k in ZSTEPS]

    share = degrees // bands
    partial_sums = call(
        legendre_kernel, shape((bands, rows, share), bf16), sums[0], *got, legendre,
        scratch=[pltpu.VMEM((rows, degrees), f32)],
    )
    parts = lax.all_to_all(partial_sums, "lat", 0, 0, tiled=True)
    return call(sum_kernel, shape((num_tapers, own_orders, 2, share), f32), parts, us=1)


def solution(mesh):
    def body(field, tapers, orders, legendre):
        return per_device(mesh.shape["lat"], field, tapers, orders, legendre)

    return jax.shard_map(
        body,
        mesh=mesh,
        in_specs=(P("lat", "lon"), P(None, "lat", "lon"), P(), P("lon", "lat", None)),
        out_specs=P(None, "lon", None, "lat"),
        check_vma=False,
    )
```

```python
import functools
import math

import jax
import jax.numpy as jnp
from jax import lax
from jax.experimental import pallas as pl
from jax.experimental.pallas import tpu as pltpu
from jax.sharding import PartitionSpec as P

NLON = 8192
CORES = 2
SIDE = 4
FIRST = ((2, 3, 1), (2, 3, 1))
SECOND = ((2, 3, 1), (2, 3, 1))
VMEM_BYTES = 12 * 1024 * 1024
SIN = [(-1.0) ** n / math.factorial(2 * n + 1) for n in range(6)]


def step_of(steps, core, n):
    return sum(jnp.where((n == at + 1) & (core == c), steps[c][at], 0) for c in range(CORES) for at in range(3))


def step_to(z, y, core, first, second):
    first, second = step_of(FIRST, core, first), step_of(SECOND, core, second)
    along_y = jnp.where(core == 0, first, second)
    return z ^ first ^ second ^ along_y, y ^ along_y


def contract_last(a, b):
    return lax.dot_general(a, b, (((1,), (1,)), ((), ())), preferred_element_type=jnp.float32)


def taper(field, tapers, k):
    return (field[...] * tapers[k].astype(jnp.float32)).astype(jnp.bfloat16)


def first_kernel(field, tapers, orders, out, orders_here, field_here, tapers_here, sems):
    parts = [(field, field_here)] + [(tapers.at[k], tapers_here.at[k]) for k in range(out.shape[0])] + [(orders, orders_here)]
    copies = [pltpu.make_async_copy(a, b, sems.at[n]) for n, (a, b) in enumerate(parts)]
    for copy in copies:
        copy.start()
    copies[0].wait()
    for k in range(out.shape[0]):
        copies[1 + k].wait()
        out[k] = taper(field_here, tapers_here, k)
    copies[-1].wait()


def trig_kernel(orders, own, other):
    rows, lons = own.shape
    me = lax.axis_index("lon")
    z, y, core = me // (SIDE * CORES), me // CORES % SIDE, me % CORES
    row = lax.broadcasted_iota(jnp.int32, (rows, orders.shape[1]), 0)
    lane = lax.broadcasted_iota(jnp.int32, (rows, orders.shape[1]), 1)
    to_z, to_y = step_to(z, y, core, row // 32, row // 8 % SIDE)
    slot = ((to_z * SIDE + to_y) * CORES + core) * 4 + row // 2 % 4
    picked = jnp.where(lane == slot, orders[...].astype(jnp.float32), 0.0)
    order = jnp.sum(picked, axis=1, keepdims=True).astype(jnp.int32)
    quarter = lax.broadcasted_iota(jnp.int32, (rows, lons), 0) % 2 * (NLON // 4)
    step = lax.broadcasted_iota(jnp.int32, (rows, lons), 1)
    for out, sector in ((own, me), (other, me ^ 1)):
        turn = (order * (sector * lons + step) + quarter) & (NLON - 1)
        arc = (NLON // 4 - jnp.minimum(turn, NLON - turn)).astype(jnp.float32) * (2.0 * math.pi / NLON)
        square = arc * arc
        value = jnp.full_like(arc, SIN[-1])
        for c in SIN[-2::-1]:
            value = value * square + c
        out[...] = (value * arc).astype(out.dtype)


def blocks(trig, tapered):
    parts = [contract_last(trig[...], t).reshape(SIDE * SIDE, -1, t.shape[0]) for t in tapered]
    return jnp.concatenate(parts, axis=1)


def own_kernel(trig, tapered, out):
    for pair in range(tapered.shape[0] // 2):
        out[:, pair * 16:pair * 16 + 16, :] = blocks(trig, [tapered[2 * pair + k] for k in range(2)])


def other_kernel(trig, field, tapers, acc, *outs):
    for pair in range(tapers.shape[0] // 2):
        tapered = [taper(field, tapers, 2 * pair + k) for k in range(2)]
        rows = slice(pair * 16, pair * 16 + 16)
        block = blocks(trig, tapered) + acc[:, rows, :]
        for k, out in enumerate(outs):
            out[:, rows, :] = block[SIDE * k:SIDE * k + SIDE].astype(out.dtype)


def add_kernel(own, *refs):
    got, outs = refs[:-SIDE], refs[-SIDE:]
    total = own[...]
    for piece in got:
        total = total + piece[...].astype(jnp.float32)
    for k, out in enumerate(outs):
        out[...] = total[k].astype(out.dtype)


def legendre_kernel(own, *refs):
    got, (legendre, out, whole) = refs[:-3], refs[-3:]
    orders, _, degrees = legendre.shape
    total = own[...]
    for piece in got:
        total = total + piece[...].astype(jnp.float32)
    slot = lax.broadcasted_iota(jnp.int32, total.shape, 0) // 2 % orders
    left = jnp.concatenate([jnp.where(slot == i, total, 0.0).astype(jnp.bfloat16) for i in range(orders)], axis=1)
    width = 768
    for at in range(0, degrees, width):
        right = legendre[:, :, at:at + width].reshape(-1, width)
        whole[:, at:at + width] = jnp.dot(left, right, preferred_element_type=jnp.float32)
    share = out.shape[2]
    for band in range(out.shape[0]):
        out[band] = whole[:, band * share:(band + 1) * share].astype(out.dtype)


def sum_kernel(parts, out):
    total = jnp.sum(parts[...].astype(jnp.float32), axis=0)
    for k in range(out.shape[0]):
        for i in range(out.shape[1]):
            row = 2 * (k * out.shape[1] + i)
            out[k, i] = total[row:row + 2, :]


def call(kernel, out_shape, *operands, scratch=(), us=2, space=pltpu.VMEM):
    spec = pl.BlockSpec(memory_space=pltpu.VMEM)
    return pl.pallas_call(
        kernel,
        out_shape=out_shape,
        in_specs=[pl.BlockSpec(memory_space=space)] * len(operands),
        out_specs=[spec] * len(out_shape) if isinstance(out_shape, list) else spec,
        scratch_shapes=list(scratch),
        compiler_params=pltpu.CompilerParams(vmem_limit_bytes=VMEM_BYTES),
        cost_estimate=pl.CostEstimate(flops=us * 10**9, bytes_accessed=us * 3 * 10**6, transcendentals=0),
    )(*operands)


def move(z, y, core, along_y, step):
    return (z, y ^ step, core) if core == along_y else (z ^ step, y, core)


def pairs(step):
    at = lambda z, y, c: (z * SIDE + y) * CORES + c
    return [(at(z, y, c), at(*step(z, y, c))) for z in range(SIDE) for y in range(SIDE) for c in range(CORES)]


def per_device(bands, field, tapers, orders, legendre):
    num_tapers, lats, lons = tapers.shape
    own_orders, _, degrees = legendre.shape
    rows = num_tapers * own_orders * 2
    shape = jax.ShapeDtypeStruct
    bf16, f32 = jnp.bfloat16, jnp.float32

    wide = shape((SIDE * SIDE * own_orders * 2, lons), bf16)
    other = [lax.ppermute(a, "lon", pairs(lambda z, y, c: (z, y, 1 - c))) for a in (field, tapers)]
    tapered, orders = call(
        first_kernel, [shape(tapers.shape, bf16), shape((1, orders.shape[0]), jnp.int32)],
        *[pltpu.with_memory_space_constraint(a, pltpu.HBM) for a in (field, tapers, orders.reshape(1, -1))],
        scratch=[
            pltpu.VMEM(field.shape, f32), pltpu.VMEM(tapers.shape, bf16), pltpu.SemaphoreType.DMA((2 + num_tapers,)),
        ],
        us=1, space=pltpu.HBM,
    )
    trig_own, trig_other = call(trig_kernel, [wide, wide], orders, us=1)
    acc = call(own_kernel, shape((SIDE * SIDE, rows, lats), f32), trig_own, tapered, us=1)
    plane = (SIDE, rows, lats)
    sums = call(other_kernel, [shape(plane, f32)] + [shape(plane, bf16)] * 3, trig_other, *other, acc, us=1)
    got = [lax.ppermute(sums[n], "lon", pairs(lambda z, y, c: move(z, y, c, 0, FIRST[c][n - 1]))) for n in range(1, SIDE)]
    block = (rows, lats)
    sums = call(add_kernel, [shape(block, f32)] + [shape(block, bf16)] * 3, sums[0], *got, us=1)
    got = [lax.ppermute(sums[n], "lon", pairs(lambda z, y, c: move(z, y, c, 1, SECOND[c][n - 1]))) for n in range(1, SIDE)]

    share = degrees // bands
    partial_sums = call(
        legendre_kernel, shape((bands, rows, share), bf16), sums[0], *got, legendre,
        scratch=[pltpu.VMEM((rows, degrees), f32)],
    )
    parts = lax.all_to_all(partial_sums, "lat", 0, 0, tiled=True)
    return call(sum_kernel, shape((num_tapers, own_orders, 2, share), f32), parts, us=1)


def solution(mesh):
    def body(field, tapers, orders, legendre):
        return per_device(mesh.shape["lat"], field, tapers, orders, legendre)

    return jax.shard_map(
        body,
        mesh=mesh,
        in_specs=(P("lat", "lon"), P(None, "lat", "lon"), P(), P("lon", "lat", None)),
        out_specs=P(None, "lon", None, "lat"),
        check_vma=False,
    )
```

```python
import functools
import math

import jax
import jax.numpy as jnp
from jax import lax
from jax.experimental import pallas as pl
from jax.experimental.pallas import tpu as pltpu
from jax.sharding import PartitionSpec as P

NLON = 8192
CORES = 2
SIDE = 4
FIRST = ((2, 3, 1), (2, 3, 1))
SECOND = ((2, 3, 1), (1, 3, 2))
VMEM_BYTES = 12 * 1024 * 1024
SIN = [(-1.0) ** n / math.factorial(2 * n + 1) for n in range(6)]


def step_of(steps, core, n):
    return sum(jnp.where((n == at + 1) & (core == c), steps[c][at], 0) for c in range(CORES) for at in range(3))


def step_to(z, y, core, first, second):
    first, second = step_of(FIRST, core, first), step_of(SECOND, core, second)
    along_y = jnp.where(core == 0, first, second)
    return z ^ first ^ second ^ along_y, y ^ along_y


def contract_last(a, b):
    return lax.dot_general(a, b, (((1,), (1,)), ((), ())), preferred_element_type=jnp.float32)


def taper(field, tapers, k):
    return (field[...] * tapers[k].astype(jnp.float32)).astype(jnp.bfloat16)


def first_kernel(field, tapers, orders, out, orders_here, field_here, tapers_here, sems):
    parts = [(field, field_here)] + [(tapers.at[k], tapers_here.at[k]) for k in range(out.shape[0])] + [(orders, orders_here)]
    copies = [pltpu.make_async_copy(a, b, sems.at[n]) for n, (a, b) in enumerate(parts)]
    for copy in copies:
        copy.start()
    copies[0].wait()
    for k in range(out.shape[0]):
        copies[1 + k].wait()
        out[k] = taper(field_here, tapers_here, k)
    copies[-1].wait()


def trig_kernel(orders, own, other):
    rows, lons = own.shape
    me = lax.axis_index("lon")
    z, y, core = me // (SIDE * CORES), me // CORES % SIDE, me % CORES
    row = lax.broadcasted_iota(jnp.int32, (rows, orders.shape[1]), 0)
    lane = lax.broadcasted_iota(jnp.int32, (rows, orders.shape[1]), 1)
    to_z, to_y = step_to(z, y, core, row // 32, row // 8 % SIDE)
    slot = ((to_z * SIDE + to_y) * CORES + core) * 4 + row // 2 % 4
    picked = jnp.where(lane == slot, orders[...].astype(jnp.float32), 0.0)
    order = jnp.sum(picked, axis=1, keepdims=True).astype(jnp.int32)
    quarter = lax.broadcasted_iota(jnp.int32, (rows, lons), 0) % 2 * (NLON // 4)
    step = lax.broadcasted_iota(jnp.int32, (rows, lons), 1)
    for out, sector in ((own, me), (other, me ^ 1)):
        turn = (order * (sector * lons + step) + quarter) & (NLON - 1)
        arc = (NLON // 4 - jnp.minimum(turn, NLON - turn)).astype(jnp.float32) * (2.0 * math.pi / NLON)
        square = arc * arc
        value = jnp.full_like(arc, SIN[-1])
        for c in SIN[-2::-1]:
            value = value * square + c
        out[...] = (value * arc).astype(out.dtype)


def blocks(trig, tapered):
    parts = [contract_last(trig[...], t).reshape(SIDE * SIDE, -1, t.shape[0]) for t in tapered]
    return jnp.concatenate(parts, axis=1)


def own_kernel(trig, tapered, out):
    for pair in range(tapered.shape[0] // 2):
        out[:, pair * 16:pair * 16 + 16, :] = blocks(trig, [tapered[2 * pair + k] for k in range(2)])


def other_kernel(trig, field, tapers, acc, *outs):
    for pair in range(tapers.shape[0] // 2):
        tapered = [taper(field, tapers, 2 * pair + k) for k in range(2)]
        rows = slice(pair * 16, pair * 16 + 16)
        block = blocks(trig, tapered) + acc[:, rows, :]
        for k, out in enumerate(outs):
            out[:, rows, :] = block[SIDE * k:SIDE * k + SIDE].astype(out.dtype)


def add_kernel(own, *refs):
    got, outs = refs[:-SIDE], refs[-SIDE:]
    total = own[...]
    for piece in got:
        total = total + piece[...].astype(jnp.float32)
    for k, out in enumerate(outs):
        out[...] = total[k].astype(out.dtype)


def legendre_kernel(own, *refs):
    got, (legendre, out, whole) = refs[:-3], refs[-3:]
    orders, _, degrees = legendre.shape
    total = own[...]
    for piece in got:
        total = total + piece[...].astype(jnp.float32)
    slot = lax.broadcasted_iota(jnp.int32, total.shape, 0) // 2 % orders
    left = jnp.concatenate([jnp.where(slot == i, total, 0.0).astype(jnp.bfloat16) for i in range(orders)], axis=1)
    width = 2304
    for at in range(0, degrees, width):
        right = legendre[:, :, at:at + width].reshape(-1, width)
        whole[:, at:at + width] = jnp.dot(left, right, preferred_element_type=jnp.float32)
    share = out.shape[2]
    for band in range(out.shape[0]):
        out[band] = whole[:, band * share:(band + 1) * share].astype(out.dtype)


def sum_kernel(parts, out):
    total = jnp.sum(parts[...].astype(jnp.float32), axis=0)
    for k in range(out.shape[0]):
        for i in range(out.shape[1]):
            row = 2 * (k * out.shape[1] + i)
            out[k, i] = total[row:row + 2, :]


def call(kernel, out_shape, *operands, scratch=(), us=2, space=pltpu.VMEM):
    spec = pl.BlockSpec(memory_space=pltpu.VMEM)
    return pl.pallas_call(
        kernel,
        out_shape=out_shape,
        in_specs=[pl.BlockSpec(memory_space=space)] * len(operands),
        out_specs=[spec] * len(out_shape) if isinstance(out_shape, list) else spec,
        scratch_shapes=list(scratch),
        compiler_params=pltpu.CompilerParams(vmem_limit_bytes=VMEM_BYTES),
        cost_estimate=pl.CostEstimate(flops=us * 10**9, bytes_accessed=us * 3 * 10**6, transcendentals=0),
    )(*operands)


def move(z, y, core, along_y, step):
    return (z, y ^ step, core) if core == along_y else (z ^ step, y, core)


def pairs(step):
    at = lambda z, y, c: (z * SIDE + y) * CORES + c
    return [(at(z, y, c), at(*step(z, y, c))) for z in range(SIDE) for y in range(SIDE) for c in range(CORES)]


def per_device(bands, field, tapers, orders, legendre):
    num_tapers, lats, lons = tapers.shape
    own_orders, _, degrees = legendre.shape
    rows = num_tapers * own_orders * 2
    shape = jax.ShapeDtypeStruct
    bf16, f32 = jnp.bfloat16, jnp.float32

    wide = shape((SIDE * SIDE * own_orders * 2, lons), bf16)
    other = [lax.ppermute(a, "lon", pairs(lambda z, y, c: (z, y, 1 - c))) for a in (field, tapers)]
    tapered, orders = call(
        first_kernel, [shape(tapers.shape, bf16), shape((1, orders.shape[0]), jnp.int32)],
        *[pltpu.with_memory_space_constraint(a, pltpu.HBM) for a in (field, tapers, orders.reshape(1, -1))],
        scratch=[
            pltpu.VMEM(field.shape, f32), pltpu.VMEM(tapers.shape, bf16), pltpu.SemaphoreType.DMA((2 + num_tapers,)),
        ],
        us=1, space=pltpu.HBM,
    )
    trig_own, trig_other = call(trig_kernel, [wide, wide], orders, us=1)
    acc = call(own_kernel, shape((SIDE * SIDE, rows, lats), f32), trig_own, tapered, us=1)
    plane = (SIDE, rows, lats)
    sums = call(other_kernel, [shape(plane, f32)] + [shape(plane, bf16)] * 3, trig_other, *other, acc, us=1)
    got = [lax.ppermute(sums[n], "lon", pairs(lambda z, y, c: move(z, y, c, 0, FIRST[c][n - 1]))) for n in range(1, SIDE)]
    block = (rows, lats)
    sums = call(add_kernel, [shape(block, f32)] + [shape(block, bf16)] * 3, sums[0], *got, us=12)
    got = [lax.ppermute(sums[n], "lon", pairs(lambda z, y, c: move(z, y, c, 1, SECOND[c][n - 1]))) for n in range(1, SIDE)]

    share = degrees // bands
    partial_sums = call(
        legendre_kernel, shape((bands, rows, share), bf16), sums[0], *got, legendre,
        scratch=[pltpu.VMEM((rows, degrees), f32)],
    )
    parts = lax.all_to_all(partial_sums, "lat", 0, 0, tiled=True)
    return call(sum_kernel, shape((num_tapers, own_orders, 2, share), f32), parts, us=1)


def solution(mesh):
    def body(field, tapers, orders, legendre):
        return per_device(mesh.shape["lat"], field, tapers, orders, legendre)

    return jax.shard_map(
        body,
        mesh=mesh,
        in_specs=(P("lat", "lon"), P(None, "lat", "lon"), P(), P("lon", "lat", None)),
        out_specs=P(None, "lon", None, "lat"),
        check_vma=False,
    )
```
